256 devices in a mesh: mp: 4 (over z_lo), proj: 64 (over x, y, z_hi, core).
Axes of the slice: x: 4, y: 4, z: 8 (z_hi: 2, z_lo: 4; z = z_hi * 4 + z_lo), core: 2. Of those that a mesh axis runs over, the one named last changes fastest.
Arguments:
- normed_hidden_input: bfloat16 [8192, 5120], P('proj', 'mp'), may hold values from -6 to 6
- attention_mixture: bfloat16 [8192, 5120], P('proj', 'mp'), may hold values from -6 to 6
- normed_gate_input: bfloat16 [8192, 5120], P('proj', 'mp'), may hold values from -6 to 6
- down_projection_input: bfloat16 [8192, 27648], P('proj', 'mp'), may hold values from -6 to 6
- query_out_cotangent: bfloat16 [8192, 5120], P('proj', 'mp'), may hold values from -6 to 6
- key_value_cotangents: bfloat16 [8192, 2, 1024], P('proj', None, 'mp'), may hold values from -6 to 6
- attention_out_cotangent: bfloat16 [8192, 5120], P('proj', 'mp'), may hold values from -6 to 6
- gate_up_cotangents: bfloat16 [8192, 2, 27648], P('proj', None, 'mp'), may hold values from -6 to 6
- down_out_cotangent: bfloat16 [8192, 5120], P('proj', 'mp'), may hold values from -6 to 6
- adapter_input_factors: bfloat16 [6, 8, 5120], P(None, None, 'mp'), may hold values from -0.078125 to 0.078125
- down_adapter_input_factor: bfloat16 [8, 27648], P(None, 'mp'), may hold values from -0.0390625 to 0.0390625
- adapter_output_factors: bfloat16 [3, 8, 5120], P(None, None, 'mp'), may hold values from -0.078125 to 0.078125
- key_value_adapter_output: bfloat16 [2, 8, 1024], P(None, None, 'mp'), may hold values from -0.1875 to 0.1875
- gate_up_adapter_output: bfloat16 [2, 8, 27648], P(None, None, 'mp'), may hold values from -0.0390625 to 0.0390625
- verified_loss_mask: int32 [8192], P('proj'), may hold values 0 or 1
- block_projector_seeds: int32 [14], replicated, may hold values from 0 to 16777215
Outputs:
- features: float32 [4, 2048], P(None, ('mp', 'proj'))
The draws below stay inside these ranges and needn't reach their ends.
All inputs are finite; a program needn't handle non-finite values. No bound on the sum of `verified_loss_mask` on one device may be relied on, other than what follows from the above.
Results may differ from the reference program's by a relative error of at most 0.0028.
Values sent between devices are 32-bit elements; how exact they have to be, the bound alone decides.
A program may use at most 64 MiB of HBM per device.

```python
import math
import jax
import jax.numpy as jnp
from jax import lax

MODEL_WIDTH = 5120
FEEDFORWARD_UNITS = 27648
KEY_WIDTH = 1024
ADAPTER_RANK = 8
K = 2048
LENGTH = 2048
SEGS = 14
TOKENS = 8192
EXAMPLES = 4


def touch_ends(result, key, low, largest):
    spot = [jax.random.randint(jax.random.fold_in(key, axis), (), 0, length) for axis, length in enumerate(result.shape)]
    main_axis = result.shape.index(max(result.shape))
    neighbour = spot[:main_axis] + [(spot[main_axis] + 1) % result.shape[main_axis]] + spot[main_axis + 1:]
    return result.at[tuple(spot)].set(low).at[tuple(neighbour)].set(largest)


def steps_of(rng, shape, pieces, least, top_value):
    loudness = 1.0
    for dim, shards_of in pieces:
        steps = jax.random.uniform(jax.random.fold_in(jax.random.fold_in(rng, 6), dim), (shards_of,), jnp.float32, least / len(pieces), top_value / len(pieces))
        loudness = loudness * jnp.repeat(jnp.exp(steps), shape[dim] // shards_of).reshape((-1,) + (1,) * (len(shape) - 1 - dim))
    return loudness


def gaussian(own_key, extent, width, reach, shards=(), kind=jnp.bfloat16):
    values = jax.random.normal(own_key, extent, jnp.float32) * width
    if len(shards) > 0:
        values = steps_of(own_key, extent, shards, -0.22, 0.18) * values
    return jnp.clip(values, min=-reach, max=reach).astype(kind)


def setup_inputs(seed: int = 0) -> dict:
    splits = jax.random.split(jax.random.key(seed), 17)
    normed_hidden_input = gaussian(splits[0], (TOKENS, MODEL_WIDTH), 1.0, 6.0, ((0, 64), (1, 4)))
    attention_mixture = gaussian(splits[1], (TOKENS, MODEL_WIDTH), 1.0, 6.0, ((0, 64), (1, 4)))
    normed_gate_input = gaussian(splits[2], (TOKENS, MODEL_WIDTH), 1.0, 6.0, ((0, 64), (1, 4)))
    down_projection_input = gaussian(splits[3], (TOKENS, FEEDFORWARD_UNITS), 1.0, 6.0, ((0, 64), (1, 4)))
    query_out_cotangent = gaussian(splits[4], (TOKENS, MODEL_WIDTH), 1.0, 6.0, ((0, 64), (1, 4)))
    key_value_cotangents = gaussian(splits[5], (TOKENS, 2, KEY_WIDTH), 1.0, 6.0, ((0, 64), (2, 4)))
    attention_out_cotangent = gaussian(splits[6], (TOKENS, MODEL_WIDTH), 1.0, 6.0, ((0, 64), (1, 4)))
    gate_up_cotangents = gaussian(splits[7], (TOKENS, 2, FEEDFORWARD_UNITS), 1.0, 6.0, ((0, 64), (2, 4)))
    down_out_cotangent = gaussian(splits[8], (TOKENS, MODEL_WIDTH), 1.0, 6.0, ((0, 64), (1, 4)))
    adapter_input_factors = gaussian(splits[9], (6, ADAPTER_RANK, MODEL_WIDTH), MODEL_WIDTH ** -0.5, 0.078125, ((2, 4),))
    down_adapter_input_factor = gaussian(splits[10], (ADAPTER_RANK, FEEDFORWARD_UNITS), FEEDFORWARD_UNITS ** -0.5, 0.0390625, ((1, 4),))
    adapter_output_factors = gaussian(splits[11], (3, ADAPTER_RANK, MODEL_WIDTH), MODEL_WIDTH ** -0.5, 0.078125, ((2, 4),))
    key_value_adapter_output = gaussian(splits[12], (2, ADAPTER_RANK, KEY_WIDTH), KEY_WIDTH ** -0.5, 0.1875, ((2, 4),))
    gate_up_adapter_output = gaussian(splits[13], (2, ADAPTER_RANK, FEEDFORWARD_UNITS), FEEDFORWARD_UNITS ** -0.5, 0.0390625, ((2, 4),))
    verified_loss_mask = touch_ends((jax.random.randint(splits[14], (TOKENS,), 0, 4) < 3).astype(jnp.int32), jax.random.fold_in(splits[14], 1), 0, 1)
    block_projector_seeds = touch_ends(jax.random.randint(splits[15], (SEGS,), 0, 16777216), jax.random.fold_in(splits[15], 1), 0, 16777215).astype(jnp.int32)
    return dict(normed_hidden_input=normed_hidden_input, attention_mixture=attention_mixture, normed_gate_input=normed_gate_input, down_projection_input=down_projection_input, query_out_cotangent=query_out_cotangent, key_value_cotangents=key_value_cotangents, attention_out_cotangent=attention_out_cotangent, gate_up_cotangents=gate_up_cotangents, down_out_cotangent=down_out_cotangent, adapter_input_factors=adapter_input_factors, down_adapter_input_factor=down_adapter_input_factor, adapter_output_factors=adapter_output_factors, key_value_adapter_output=key_value_adapter_output, gate_up_adapter_output=gate_up_adapter_output, verified_loss_mask=verified_loss_mask, block_projector_seeds=block_projector_seeds)


def mix_bits(row_keys, col_keys):
    hashed = row_keys[:, None] ^ col_keys[None, :]
    hashed = hashed ^ hashed >> 16 & 65535
    hashed = hashed * -2048144789
    hashed = hashed ^ hashed >> 13 & 524287
    hashed = hashed * -1028477387
    hashed = hashed ^ hashed >> 16 & 65535
    byte_sum = (hashed & 255) + (hashed >> 8 & 255) + (hashed >> 16 & 255) + (hashed >> 24 & 255)
    return (byte_sum - 510).astype(jnp.float32)

def project_rows(gradients, row_keys, col_keys, block_limit):
    row_count = gradients.shape[1]
    block_rows = math.gcd(row_count, block_limit)

    def add_block(number, accumulated):
        first_row = (number * block_rows).astype(jnp.int32)
        grad_block = lax.dynamic_slice_in_dim(gradients, first_row, block_rows, 1)
        key_block = lax.dynamic_slice_in_dim(row_keys, first_row, block_rows, 0)
        table = mix_bits(key_block, col_keys)
        return accumulated + jnp.dot(grad_block, table, precision=lax.Precision.HIGHEST, preferred_element_type=jnp.float32)
    zero_acc = jnp.zeros((gradients.shape[0], col_keys.shape[0]), jnp.float32)
    return lax.fori_loop(0, row_count // block_rows, add_block, zero_acc)

def segment_keys(seg_width, seed_value):
    positions = jnp.arange(ADAPTER_RANK * seg_width, dtype=jnp.int32)
    rank_pos = positions // seg_width
    feature = positions % seg_width
    return seed_value * 1103515245 + (feature * ADAPTER_RANK + rank_pos) * 668265263

def example_grads(inputs, cotangent, factor_a, factor_b, weights):
    act_a = jnp.dot(inputs, factor_a.T, preferred_element_type=jnp.float32)
    act_b = jnp.dot(cotangent, factor_b.T, preferred_element_type=jnp.float32)
    masked_v = (weights * act_a).astype(jnp.bfloat16)
    masked_u = (weights * act_b).astype(jnp.bfloat16)
    in_width = inputs.shape[1]
    out_width = cotangent.shape[1]

    def one_rollout(packed):
        rollout_in, rollout_cot, rollout_u, rollout_v = packed
        grad_a = jnp.dot(rollout_u.T, rollout_in, preferred_element_type=jnp.float32)
        grad_b = jnp.dot(rollout_v.T, rollout_cot, preferred_element_type=jnp.float32)
        return (grad_a.reshape(-1), grad_b.reshape(-1))
    return lax.map(one_rollout, (inputs.reshape(EXAMPLES, LENGTH, in_width), cotangent.reshape(EXAMPLES, LENGTH, out_width), masked_u.reshape(EXAMPLES, LENGTH, ADAPTER_RANK), masked_v.reshape(EXAMPLES, LENGTH, ADAPTER_RANK)))

def reference(normed_hidden_input, attention_mixture, normed_gate_input, down_projection_input, query_out_cotangent, key_value_cotangents, attention_out_cotangent, gate_up_cotangents, down_out_cotangent, adapter_input_factors, down_adapter_input_factor, adapter_output_factors, key_value_adapter_output, gate_up_adapter_output, verified_loss_mask, block_projector_seeds):
    weights = verified_loss_mask.astype(jnp.float32)[:, None]
    block_triplets = [(normed_hidden_input, query_out_cotangent, adapter_input_factors[0], adapter_output_factors[0]), (normed_hidden_input, key_value_cotangents[:, 0], adapter_input_factors[1], key_value_adapter_output[0]), (normed_hidden_input, key_value_cotangents[:, 1], adapter_input_factors[2], key_value_adapter_output[1]), (attention_mixture, attention_out_cotangent, adapter_input_factors[3], adapter_output_factors[1]), (normed_gate_input, gate_up_cotangents[:, 0], adapter_input_factors[4], gate_up_adapter_output[0]), (normed_gate_input, gate_up_cotangents[:, 1], adapter_input_factors[5], gate_up_adapter_output[1]), (down_projection_input, down_out_cotangent, down_adapter_input_factor, adapter_output_factors[2])]
    col_keys = jnp.arange(K, dtype=jnp.int32) * -1640531535
    raw_sum = jnp.zeros((EXAMPLES, K), jnp.float32)
    for number, (inputs, cotangent, factor_a, factor_b) in enumerate(block_triplets):
        grad_a, grad_b = example_grads(inputs, cotangent, factor_a, factor_b, weights)
        keys_a = segment_keys(inputs.shape[1], block_projector_seeds[2 * number])
        keys_b = segment_keys(cotangent.shape[1], block_projector_seeds[2 * number + 1])
        raw_sum = raw_sum + project_rows(grad_a, keys_a, col_keys, 1024)
        raw_sum = raw_sum + project_rows(grad_b, keys_b, col_keys, 1024)
    scale_out = 1.0 / (LENGTH * math.sqrt(21845.0 * K))
    return raw_sum * scale_out
```

```python
import functools
import math

import jax
import jax.numpy as jnp
from jax import lax
from jax.experimental import pallas as pl
from jax.experimental.pallas import tpu as pltpu
from jax.sharding import PartitionSpec as P

K = 2048
LENGTH = 2048
LANES = 128
MESH = pl.DeviceIdType.MESH
F32, BF16, I32 = jnp.float32, jnp.bfloat16, jnp.int32


def wrap(value):
    return (value + 2**31) % 2**32 - 2**31


M1, M2 = -2048144789, -1028477387
SEED_STEP, ROW_STEP, COL_STEP = 1103515245, 668265263, -1640531535

CHUNKS = (
    ((12, 54), (13, 10)),
    ((8, 10), (9, 54)),
    ((10, 10), (11, 54)),
    ((0, 10), (1, 10), (2, 10), (3, 2), (4, 10), (5, 2), (6, 10), (7, 10)),
)
GROUPS = ((0, 2), (2, 4), (6, 8))
ROWS = 32
STEPS = 4096 // ROWS


def srl(value, count):
    return lax.shift_right_logical(value, jnp.int32(count))


def nt(a, b):
    return lax.dot_general(a, b, (((1,), (1,)), ((), ())), preferred_element_type=F32)


def nn(a, b):
    return jnp.dot(a, b, preferred_element_type=F32)


def kernel(
    xh_in, xo_in, xg_in, xd_in, gq_in, kv_in, go_in, gu_in, gd_in, ai_in, ad_in, ao_in, kvb_in, gub_in, mask_in, seed_in,
    out_ref,
    xh, xo, xg, xd, gq, kv, go, gu, gd, ai, ad, ao, kvb, gub, mask, seed,
    key_base, col_key, table, part, part_in, grads, core_in, half, y_in, quarter, z_in, lhs, total, a_out, a_in, b_in,
    load_sem, mp_send, mp_recv, core_send, core_recv, y_send, y_recv, z_send, z_recv, fin_send, fin_recv,
):
    mp = lax.axis_index("mp")
    proj = lax.axis_index("proj")
    x, y, zh, core = proj // 16, (proj // 4) % 4, (proj // 2) % 2, proj % 2

    def device(x, y, zh, core, mp):
        return {"mp": mp, "proj": x * 16 + y * 4 + zh * 2 + core}

    def turn(value, by, size):
        return (value + by) % size

    plane = [(dx, dy) for dx in range(4) for dy in range(4) if dx or dy]
    column = [(dm, dz, dc) for dm in range(4) for dz in range(2) for dc in range(2) if dm or dz or dc]
    cross = [(dx, dz) for dx in range(4) for dz in range(2) if dx or dz]
    greet = [device(turn(x, dx, 4), turn(y, dy, 4), zh, core, mp) for dx, dy in plane]
    greet += [device(x, y, turn(zh, dz, 2), turn(core, dc, 2), turn(mp, dm, 4)) for dm, dz, dc in column]
    greet += [device(turn(x, dx, 4), y, 1 - zh, core, mp) for dx in range(1, 4)]
    barrier = pltpu.get_barrier_semaphore()
    for peer in greet:
        pl.semaphore_signal(barrier, inc=1, device_id=peer, device_id_type=MESH)

    def load(number, source, target):
        pltpu.make_async_copy(source, target, load_sem.at[number]).start()

    def loaded(number, target):
        pltpu.make_async_copy(target, target, load_sem.at[number]).wait()

    load(15, seed_in, seed)
    load(10, ad_in, ad)
    load(3, xd_in, xd)
    load(11, ao_in, ao)
    load(8, gd_in, gd)
    load(13, gub_in, gub)
    for tile in range(54):
        load(7, gu_in.at[:, :, tile * LANES : (tile + 1) * LANES], gu.at[tile])
    load(9, ai_in, ai)
    load(2, xg_in, xg)
    load(0, xh_in, xh)
    load(12, kvb_in, kvb)
    for tile in range(2):
        load(5, kv_in.at[:, :, tile * LANES : (tile + 1) * LANES], kv.at[tile])
    load(4, gq_in, gq)
    load(1, xo_in, xo)
    load(6, go_in, go)
    load(14, mask_in, mask)

    place = lax.broadcasted_iota(I32, (8, K), 1)
    q, m, i = place >> 7, (place >> 3) & 15, place & 7
    col = (((m >> 2) * 64 + q * 4 + (m & 3)) * 8 + i) * COL_STEP
    col_key[...] = col ^ srl(col, 16)

    loaded(15, seed)
    block = core * 32 + y * 8 + x * 2 + zh
    for chunk, segments in enumerate(CHUNKS):
        edge = 0
        first = jnp.int32(0)
        for segment, blocks in segments:
            here = seed[segment] * SEED_STEP + (mp * blocks + block - edge) * wrap(LANES * 8 * ROW_STEP)
            first = here if edge == 0 else jnp.where(block >= edge, here, first)
            edge += blocks
        for rank in range(8):
            key_base[chunk * 8 + rank] = first + wrap(rank * ROW_STEP)

    def hash_step(step, carry):
        del carry
        base = key_base[step // (LANES // ROWS)]
        row0 = (step % (LANES // ROWS)) * ROWS
        row = base + (lax.broadcasted_iota(I32, (ROWS, LANES), 0) + row0) * wrap(8 * ROW_STEP)
        row = row ^ srl(row, 16)
        at = pl.multiple_of(step * ROWS, ROWS)
        for tile in range(K // LANES):
            lanes = slice(tile * LANES, (tile + 1) * LANES)
            key = jnp.concatenate([col_key[:, lanes]] * (ROWS // 8), axis=0)
            h = (row ^ key) * M1
            h = h ^ srl(h, 13)
            h = h * M2
            h = h ^ srl(h, 16)
            h = (h & 0x00FF00FF) + (srl(h, 8) & 0x00FF00FF)
            h = srl(h * 0x00010001, 16)
            table[pl.ds(at, ROWS), lanes] = (h.astype(F32) - 510.0).astype(BF16)
        return 0

    done = [0]

    def hash_rows(until):
        if until > done[0]:
            lax.fori_loop(done[0], until, hash_step, 0)
            done[0] = until

    pair = lax.broadcasted_iota(I32, (2 * LANES, LANES), 0)
    token = lax.broadcasted_iota(I32, (2 * LANES, LANES), 1)
    pick = [(pair == 2 * token + j).astype(F32).astype(BF16) for j in range(2)]
    odd = (lax.broadcasted_iota(I32, (8, 2 * LANES), 1) & 1) == 1

    def remote(source, target, send, recv, peer):
        pltpu.make_async_remote_copy(
            src_ref=source, dst_ref=target, send_sem=send, recv_sem=recv, device_id=peer, device_id_type=MESH
        ).start()

    def wait_for(ref, sem):
        pltpu.make_async_copy(ref, ref, sem).wait()

    def paired(buffer, tile):
        return jnp.concatenate(
            [buffer.at[tile].reshape(2 * LANES, LANES)[...], buffer.at[tile + 1].reshape(2 * LANES, LANES)[...]], axis=1
        )

    def send_part(group):
        start, size = GROUPS[group]
        for step in range(1, 4):
            remote(
                part.at[pl.ds(start, size)], part_in.at[step - 1, pl.ds(start, size)], mp_send.at[group], mp_recv.at[group],
                device(x, y, zh, core, turn(mp, step, 4)),
            )

    def factor_products(group):
        if group == 0:
            for number, ref in ((10, ad), (3, xd), (11, ao), (8, gd)):
                loaded(number, ref)
            part[0] = nt(ad[...], xd[...])
            part[1] = nt(ao[2], gd[...])
        elif group == 1:
            for number, ref in ((13, gub), (7, gu), (9, ai), (2, xg)):
                loaded(number, ref)
            both = nt(jnp.concatenate([ai[4], ai[5]], axis=0), xg[...])
            part[2] = both[:8]
            part[3] = both[8:]
            acc = jnp.zeros((16, 2 * LANES), F32)
            for tile in range(0, 54, 2):
                lanes = slice(tile * LANES, (tile + 2) * LANES)
                acc += nt(jnp.concatenate([gub[0, :, lanes], gub[1, :, lanes]], axis=0), paired(gu, tile))
            both = jnp.where(odd, acc[8:], acc[:8])
            part[4] = both[:, :LANES]
            part[5] = both[:, LANES:]
        else:
            for number, ref in ((0, xh), (12, kvb), (5, kv), (4, gq), (1, xo), (6, go)):
                loaded(number, ref)
            three = nt(jnp.concatenate([ai[0], ai[1], ai[2]], axis=0), xh[...])
            for j in range(3):
                part[6 + j] = three[8 * j : 8 * j + 8]
            part[9] = nt(ai[3], xo[...])
            part[10] = nt(ao[0], gq[...])
            part[11] = nt(ao[1], go[...])
            acc = nt(jnp.concatenate([kvb[0], kvb[1]], axis=0), paired(kv, 0))
            both = jnp.where(odd, acc[8:], acc[:8])
            part[12] = both[:, :LANES]
            part[13] = both[:, LANES:]
        send_part(group)

    def put(chunk, at, value):
        for tile in range(value.shape[1] // LANES):
            grads[chunk, at + tile] = value[:, tile * LANES : (tile + 1) * LANES]

    def put_wide(chunk, at, left, right):
        for start in range(0, right.shape[1], 1280):
            width = min(1280, right.shape[1] - start)
            put(chunk, at + start // LANES, nn(left, right[:, start : start + width]))

    def send_core(chunk):
        remote(
            grads.at[chunk, pl.ds((1 - core) * 32, 32)], core_in.at[chunk], core_send.at[chunk], core_recv.at[chunk],
            device(x, y, zh, 1 - core, mp),
        )

    def token_sums(group):
        start, size = GROUPS[group]
        region = part_in.at[:, pl.ds(start, size)]
        wait_for(region, mp_recv.at[group])
        if group == 0:
            loaded(14, mask)
        weights = mask[...].astype(F32)

        def tile(number):
            return (part[number] + part_in[0, number]) + (part_in[1, number] + part_in[2, number])

        def masked(number):
            return (weights * tile(number)).astype(BF16)

        def unmix(number):
            mixed = jnp.concatenate([tile(number), tile(number + 1)], axis=1).astype(BF16)
            return [(weights * nn(mixed, pick[j])).astype(BF16) for j in range(2)]

        def mix(values):
            return jnp.concatenate([nt(values[j], pick[j]) for j in range(2)], axis=0).astype(BF16)

        if group == 0:
            v, u = masked(0), masked(1)
            put_wide(0, 0, u, xd)
            put_wide(0, 54, v, gd)
            send_core(0)
        elif group == 1:
            v = mix([masked(2), masked(3)])
            u = jnp.concatenate(unmix(4), axis=0)
            both = nn(u, xg[...])
            put(1, 0, both[:8])
            put(2, 0, both[8:])
            for t in range(0, 54, 2):
                both = nn(v, paired(gu, t))
                put(1, 10 + t, both[:8])
                put(2, 10 + t, both[8:])
            send_core(1)
            send_core(2)
        else:
            vs = [masked(6 + j) for j in range(4)]
            uq, uo = masked(10), masked(11)
            uk, uv = unmix(12)
            three = nn(jnp.concatenate([uq, uk, uv], axis=0), xh[...])
            put(3, 0, three[:8])
            put(3, 10, nn(vs[0], gq[...]))
            put(3, 20, three[8:16])
            put(3, 32, three[16:])
            both = nn(mix([vs[1], vs[2]]), paired(kv, 0))
            put(3, 30, both[:8])
            put(3, 42, both[8:])
            put(3, 44, nn(uo, xo[...]))
            put(3, 54, nn(vs[3], go[...]))
            send_core(3)

    def send_y(chunk):
        wait_for(core_in.at[chunk], core_recv.at[chunk])
        half[chunk] = grads[chunk, pl.ds(core * 32, 32)] + core_in[chunk]
        for step in (2, 1, 3):
            to = turn(y, step, 4)
            remote(
                half.at[chunk, pl.ds(to * 8, 8)], y_in.at[chunk, step - 1], y_send.at[chunk], y_recv.at[chunk],
                device(x, to, zh, core, mp),
            )

    def send_z(chunk):
        wait_for(y_in.at[chunk], y_recv.at[chunk])
        quarter[chunk] = (half[chunk, pl.ds(y * 8, 8)] + y_in[chunk, 0]) + (y_in[chunk, 1] + y_in[chunk, 2])
        for dx, dz in cross[::-1]:
            to_x, to_z = turn(x, dx, 4), turn(zh, dz, 2)
            remote(
                quarter.at[chunk, to_x * 2 + to_z], z_in.at[chunk, x * 2 + zh], z_send.at[chunk], z_recv.at[chunk],
                device(to_x, y, to_z, core, mp),
            )
        z_in[chunk, x * 2 + zh] = quarter[chunk, x * 2 + zh]

    def project(chunk):
        wait_for(z_in.at[chunk, pl.ds(0, 7)], z_recv.at[chunk])
        for example in range(4):
            g = z_in[chunk, 2 * example] + z_in[chunk, 2 * example + 1]
            lhs[chunk, pl.ds(example, 8, stride=8), :] = g
            lhs[chunk, pl.ds(4 + example, 8, stride=8), :] = g - g.astype(BF16).astype(F32)
        left = jnp.concatenate([lhs[chunk, pl.ds(8 * rank, 8), :] for rank in range(8)], axis=1).astype(BF16)
        for start in range(0, K, 512):
            product = nn(left, table[chunk * 1024 : (chunk + 1) * 1024, start : start + 512])
            lanes = slice(start, start + 512)
            if chunk == 0:
                total[:, lanes] = product
            else:
                total[:, lanes] += product

    hash_rows(12)
    pl.semaphore_wait(barrier, len(greet))
    for group in range(3):
        factor_products(group)
    hash_rows(24)
    token_sums(0)
    hash_rows(32)
    token_sums(1)
    send_y(0)
    hash_rows(40)
    send_y(1)
    send_y(2)
    token_sums(2)
    hash_rows(56)
    send_z(0)
    send_y(3)
    hash_rows(72)
    send_z(1)
    send_z(2)
    hash_rows(88)
    send_z(3)
    hash_rows(104)
    project(0)
    hash_rows(STEPS)
    for chunk in range(1, 4):
        project(chunk)

    scale_out = 1.0 / (LENGTH * math.sqrt(21845.0 * K))
    for number in range(16):
        lanes = slice(number * LANES, (number + 1) * LANES)
        a_out[number] = (total[0:4, lanes] + total[4:8, lanes]) * scale_out
    here = x * 4 + y
    for dx, dy in plane[::-1]:
        to_x, to_y = turn(x, dx, 4), turn(y, dy, 4)
        remote(
            a_out.at[to_x * 4 + to_y], a_in.at[here], fin_send.at[0], fin_recv.at[0], device(to_x, to_y, zh, core, mp)
        )
    a_in[here] = a_out[here]
    wait_for(a_in.at[pl.ds(0, 15)], fin_recv.at[0])
    there = mp * 4 + zh * 2 + core
    b_in[there] = jnp.sum(a_in[...], axis=0)
    for dm, dz, dc in column[::-1]:
        remote(
            b_in.at[there], b_in.at[there], fin_send.at[1], fin_recv.at[1],
            device(x, y, turn(zh, dz, 2), turn(core, dc, 2), turn(mp, dm, 4)),
        )
    wait_for(b_in.at[pl.ds(0, 15)], fin_recv.at[1])
    summed = jnp.sum(b_in[...], axis=0)
    out_ref[...] = pltpu.roll(summed, (LANES - there * 8) % LANES, 1)

    for group, (start, size) in enumerate(GROUPS):
        wait_for(part_in.at[:, pl.ds(start, size)], mp_send.at[group])
    for chunk in range(4):
        wait_for(core_in.at[chunk], core_send.at[chunk])
        wait_for(y_in.at[chunk], y_send.at[chunk])
        wait_for(z_in.at[chunk, pl.ds(0, 7)], z_send.at[chunk])
    wait_for(a_in.at[pl.ds(0, 15)], fin_send.at[0])
    wait_for(b_in.at[pl.ds(0, 15)], fin_send.at[1])


def shards(*args):
    args = list(args)
    args[14] = args[14].reshape(1, LANES)

    def like(number):
        return pltpu.VMEM(args[number].shape, args[number].dtype)

    scratch = [like(number) for number in range(15)]
    scratch[5] = pltpu.VMEM((2, LANES, 2, LANES), BF16)
    scratch[7] = pltpu.VMEM((54, LANES, 2, LANES), BF16)
    scratch.append(pltpu.SMEM((14,), I32))
    tile = (8, LANES)
    scratch += [
        pltpu.SMEM((32,), I32),
        pltpu.VMEM((8, K), I32),
        pltpu.VMEM((4096, K), BF16),
        pltpu.VMEM((14, *tile), F32),
        pltpu.VMEM((3, 14, *tile), F32),
        pltpu.VMEM((4, 64, *tile), F32),
        pltpu.VMEM((4, 32, *tile), F32),
        pltpu.VMEM((4, 32, *tile), F32),
        pltpu.VMEM((4, 3, 8, *tile), F32),
        pltpu.VMEM((4, 8, *tile), F32),
        pltpu.VMEM((4, 8, *tile), F32),
        pltpu.VMEM((4, 64, LANES), F32),
        pltpu.VMEM((8, K), F32),
        pltpu.VMEM((16, 4, LANES), F32),
        pltpu.VMEM((16, 4, LANES), F32),
        pltpu.VMEM((16, 4, LANES), F32),
        pltpu.SemaphoreType.DMA((16,)),
        pltpu.SemaphoreType.DMA((3,)),
        pltpu.SemaphoreType.DMA((3,)),
    ]
    scratch += [pltpu.SemaphoreType.DMA((4,)) for _ in range(6)]
    scratch += [pltpu.SemaphoreType.DMA((2,)) for _ in range(2)]
    full = pl.pallas_call(
        kernel,
        out_shape=jax.ShapeDtypeStruct((4, LANES), F32),
        in_specs=[pl.BlockSpec(memory_space=pl.ANY)] * 16,
        out_specs=pl.BlockSpec(memory_space=pltpu.VMEM),
        scratch_shapes=scratch,
        compiler_params=pltpu.CompilerParams(collective_id=0, has_side_effects=True, vmem_limit_bytes=56 * 2**20),
    )(*args)
    return full[:, :8]


def solution(mesh):
    in_specs = (
        P("proj", "mp"), P("proj", "mp"), P("proj", "mp"), P("proj", "mp"), P("proj", "mp"), P("proj", None, "mp"),
        P("proj", "mp"), P("proj", None, "mp"), P("proj", "mp"), P(None, None, "mp"), P(None, "mp"), P(None, None, "mp"),
        P(None, None, "mp"), P(None, None, "mp"), P("proj"), P(),
    )
    return jax.shard_map(shards, mesh=mesh, in_specs=in_specs, out_specs=P(None, ("mp", "proj")), check_vma=False)
```

```python
import functools
import math

import jax
import jax.numpy as jnp
from jax import lax
from jax.experimental import pallas as pl
from jax.experimental.pallas import tpu as pltpu
from jax.sharding import PartitionSpec as P

K = 2048
LENGTH = 2048
LANES = 128
MESH = pl.DeviceIdType.MESH
F32, BF16, I32 = jnp.float32, jnp.bfloat16, jnp.int32


def wrap(value):
    return (value + 2**31) % 2**32 - 2**31


M1, M2 = -2048144789, -1028477387
SEED_STEP, ROW_STEP, COL_STEP = 1103515245, 668265263, -1640531535

CHUNKS = (
    ((12, 54, 0, 54), (13, 10, 0, 10)),
    ((9, 54, 0, 27), (11, 54, 0, 27), (8, 10, 0, 10)),
    ((9, 54, 27, 27), (11, 54, 27, 27), (10, 10, 0, 10)),
    tuple((segment, blocks, 0, blocks) for segment, blocks in enumerate((10, 10, 10, 2, 10, 2, 10, 10))),
)
GROUPS = ((0, 2), (2, 4), (6, 8))
ROWS = 32
STEPS = 4096 // ROWS
GU_UNROLL = 9
MIX_LOOP = 0
MIX = (0, 0, 0, 0)


def srl(value, count):
    return lax.shift_right_logical(value, jnp.int32(count))


def nt(a, b):
    return lax.dot_general(a, b, (((1,), (1,)), ((), ())), preferred_element_type=F32)


def nn(a, b):
    return jnp.dot(a, b, preferred_element_type=F32)


def kernel(
    xh_in, xo_in, xg_in, xd_in, gq_in, kv_in, go_in, gu_in, gd_in, ai_in, ad_in, ao_in, kvb_in, gub_in, mask_in, seed_in,
    out_ref,
    xh, xo, xg, xd, gq, kv, go, gu, gd, ai, ad, ao, kvb, gub, mask, seed,
    key_base, col_key, table, part, part_in, grads, core_in, half, y_in, quarter, z_in, lhs, total, a_out, a_in, b_in,
    load_sem, mp_send, mp_recv, core_send, core_recv, y_send, y_recv, z_send, z_recv, fin_send, fin_recv, told_sem,
):
    mp = lax.axis_index("mp")
    proj = lax.axis_index("proj")
    x, y, zh, core = proj // 16, (proj // 4) % 4, (proj // 2) % 2, proj % 2

    def device(x, y, zh, core, mp):
        return {"mp": mp, "proj": x * 16 + y * 4 + zh * 2 + core}

    def turn(value, by, size):
        return (value + by) % size

    plane = [(dx, dy) for dx in range(4) for dy in range(4) if dx or dy]
    column = [(dm, dz, dc) for dm in range(4) for dz in range(2) for dc in range(2) if dm or dz or dc]
    cross = [(dx, dz) for dx in range(4) for dz in range(2) if dx or dz]
    greet = [device(x, y, zh, core, turn(mp, step, 4)) for step in range(1, 4)]
    greet += [device(x, turn(y, step, 4), zh, core, mp) for step in range(1, 4)]
    greet += [device(turn(x, step, 4), y, zh, core, mp) for step in range(1, 4)]
    greet += [device(x, y, zh, 1 - core, mp), device(x, y, 1 - zh, core, 3 - mp)]
    barrier = pltpu.get_barrier_semaphore()
    for peer in greet:
        pl.semaphore_signal(barrier, inc=1, device_id=peer, device_id_type=MESH)

    def load(number, source, target):
        pltpu.make_async_copy(source, target, load_sem.at[number]).start()

    def loaded(number, target):
        pltpu.make_async_copy(target, target, load_sem.at[number]).wait()

    load(15, seed_in, seed)
    load(10, ad_in, ad)
    load(3, xd_in, xd)
    load(11, ao_in, ao)
    load(8, gd_in, gd)
    load(13, gub_in, gub)
    for tile in range(54):
        load(7, gu_in.at[:, :, tile * LANES : (tile + 1) * LANES], gu.at[tile])
    load(9, ai_in, ai)
    load(2, xg_in, xg)
    load(0, xh_in, xh)
    load(12, kvb_in, kvb)
    for tile in range(2):
        load(5, kv_in.at[:, :, tile * LANES : (tile + 1) * LANES], kv.at[tile])
    load(4, gq_in, gq)
    load(1, xo_in, xo)
    load(6, go_in, go)
    load(14, mask_in, mask)

    place = lax.broadcasted_iota(I32, (8, K), 1)
    q, m, i = place >> 7, (place >> 3) & 15, place & 7
    col = (((m >> 2) * 64 + q * 4 + (m & 3)) * 8 + i) * COL_STEP
    col_key[...] = col ^ srl(col, 16)

    loaded(15, seed)
    block = core * 32 + y * 8 + x * 2 + zh
    for chunk, segments in enumerate(CHUNKS):
        edge = 0
        first = jnp.int32(0)
        for segment, blocks, begin, count in segments:
            here = seed[segment] * SEED_STEP + (mp * blocks + begin + block - edge) * wrap(LANES * 8 * ROW_STEP)
            first = here if edge == 0 else jnp.where(block >= edge, here, first)
            edge += count
        for rank in range(8):
            key_base[chunk * 8 + rank] = first + wrap(rank * ROW_STEP)

    def hash_step(step, carry):
        del carry
        base = key_base[step // (LANES // ROWS)]
        row0 = (step % (LANES // ROWS)) * ROWS
        row = base + (lax.broadcasted_iota(I32, (ROWS, LANES), 0) + row0) * wrap(8 * ROW_STEP)
        row = row ^ srl(row, 16)
        at = pl.multiple_of(step * ROWS, ROWS)
        for tile in range(K // LANES):
            lanes = slice(tile * LANES, (tile + 1) * LANES)
            key = jnp.concatenate([col_key[:, lanes]] * (ROWS // 8), axis=0)
            h = (row ^ key) * M1
            h = h ^ srl(h, 13)
            h = h * M2
            high = srl(h, 16).astype(jnp.int16)
            low = h.astype(jnp.int16) ^ high
            carry8 = lax.shift_right_logical(low, jnp.int16(8)) + lax.shift_right_logical(high, jnp.int16(8))
            table[pl.ds(at, ROWS), lanes] = (low + high - jnp.int16(255) * carry8 - jnp.int16(510)).astype(BF16)
        return 0

    done = [0]

    def hash_rows(until):
        if until > done[0]:
            lax.fori_loop(done[0], until, hash_step, 0)
            done[0] = until

    def hash_among(count):
        for step in range(done[0], done[0] + count):
            hash_step(step, 0)
        done[0] += count

    pair = lax.broadcasted_iota(I32, (2 * LANES, LANES), 0)
    token = lax.broadcasted_iota(I32, (2 * LANES, LANES), 1)
    pick = [(pair == 2 * token + j).astype(F32).astype(BF16) for j in range(2)]
    odd = (lax.broadcasted_iota(I32, (8, 2 * LANES), 1) & 1) == 1

    def remote(source, target, send, recv, peer):
        pltpu.make_async_remote_copy(
            src_ref=source, dst_ref=target, send_sem=send, recv_sem=recv, device_id=peer, device_id_type=MESH
        ).start()

    def wait_for(ref, sem):
        pltpu.make_async_copy(ref, ref, sem).wait()

    def paired(buffer, tile):
        return jnp.concatenate(
            [buffer.at[tile].reshape(2 * LANES, LANES)[...], buffer.at[tile + 1].reshape(2 * LANES, LANES)[...]], axis=1
        )

    def send_part(group):
        start, size = GROUPS[group]
        for step in range(1, 4):
            remote(
                part.at[pl.ds(start, size)], part_in.at[step - 1, pl.ds(start, size)], mp_send.at[group], mp_recv.at[group],
                device(x, y, zh, core, turn(mp, step, 4)),
            )

    def factor_products(group):
        if group == 0:
            for number, ref in ((10, ad), (3, xd), (11, ao), (8, gd)):
                loaded(number, ref)
            part[0] = nt(ad[...], xd[...])
            part[1] = nt(ao[2], gd[...])
        elif group == 1:
            for number, ref in ((13, gub), (7, gu), (9, ai), (2, xg)):
                loaded(number, ref)
            both = nt(jnp.concatenate([ai[4], ai[5]], axis=0), xg[...])
            part[2] = both[:8]
            part[3] = both[8:]

            begin = done[0]
            done[0] += MIX_LOOP * (27 // GU_UNROLL)

            def add(step, acc):
                for extra in range(MIX_LOOP):
                    hash_step(begin + step * MIX_LOOP + extra, 0)
                for pair_at in range(GU_UNROLL):
                    tile = (step * GU_UNROLL + pair_at) * 2
                    lanes = pl.ds(pl.multiple_of(tile * LANES, 2 * LANES), 2 * LANES)
                    acc += nt(jnp.concatenate([gub[0, :, lanes], gub[1, :, lanes]], axis=0), paired(gu, tile))
                return acc

            acc = lax.fori_loop(0, 27 // GU_UNROLL, add, jnp.zeros((16, 2 * LANES), F32))
            both = jnp.where(odd, acc[8:], acc[:8])
            part[4] = both[:, :LANES]
            part[5] = both[:, LANES:]
        else:
            for number, ref in ((0, xh), (12, kvb), (5, kv), (4, gq), (1, xo), (6, go)):
                loaded(number, ref)
            three = nt(jnp.concatenate([ai[0], ai[1], ai[2]], axis=0), xh[...])
            for j in range(3):
                part[6 + j] = three[8 * j : 8 * j + 8]
            part[9] = nt(ai[3], xo[...])
            part[10] = nt(ao[0], gq[...])
            part[11] = nt(ao[1], go[...])
            acc = nt(jnp.concatenate([kvb[0], kvb[1]], axis=0), paired(kv, 0))
            both = jnp.where(odd, acc[8:], acc[:8])
            part[12] = both[:, :LANES]
            part[13] = both[:, LANES:]

    def put(chunk, at, value):
        for tile in range(value.shape[1] // LANES):
            grads[chunk, at + tile] = value[:, tile * LANES : (tile + 1) * LANES]

    def put_wide(chunk, at, left, right):
        for start in range(0, right.shape[1], 1280):
            width = min(1280, right.shape[1] - start)
            put(chunk, at + start // LANES, nn(left, right[:, start : start + width]))

    def send_core(chunk):
        remote(
            grads.at[chunk, pl.ds((1 - core) * 32, 32)], core_in.at[chunk], core_send.at[chunk], core_recv.at[chunk],
            device(x, y, zh, 1 - core, mp),
        )

    def send_y(chunk):
        wait_for(core_in.at[chunk], core_recv.at[chunk])
        half[chunk] = grads[chunk, pl.ds(core * 32, 32)] + core_in[chunk]
        for step in (2, 1, 3):
            to = turn(y, step, 4)
            remote(
                half.at[chunk, pl.ds(to * 8, 8)], y_in.at[chunk, step - 1], y_send.at[chunk], y_recv.at[chunk],
                device(x, to, zh, core, mp),
            )

    def token_sums(group):
        start, size = GROUPS[group]
        region = part_in.at[:, pl.ds(start, size)]
        wait_for(region, mp_recv.at[group])
        if group == 0:
            loaded(14, mask)
            for step in range(1, 4):
                pl.semaphore_signal(told_sem, inc=1, device_id=device(turn(x, step, 4), y, zh, core, mp), device_id_type=MESH)
        weights = mask[...].astype(F32)

        def tile(number):
            return (part[number] + part_in[0, number]) + (part_in[1, number] + part_in[2, number])

        def masked(number):
            return (weights * tile(number)).astype(BF16)

        def unmix(number):
            mixed = jnp.concatenate([tile(number), tile(number + 1)], axis=1).astype(BF16)
            return [(weights * nn(mixed, pick[j])).astype(BF16) for j in range(2)]

        def mix(values):
            return jnp.concatenate([nt(values[j], pick[j]) for j in range(2)], axis=0).astype(BF16)

        if group == 0:
            v, u = masked(0), masked(1)
            hash_among(MIX[0])
            put_wide(0, 0, u, xd)
            put_wide(0, 54, v, gd)
            send_core(0)
        elif group == 1:
            v = mix([masked(2), masked(3)])
            u = jnp.concatenate(unmix(4), axis=0)
            both = nn(u, xg[...])
            put(1, 54, both[:8])
            put(2, 54, both[8:])
            for half in range(2):
                hash_among(MIX[1 + half])
                for t in range(0, 28, 2) if half == 0 else range(28, 54, 2):
                    both = nn(v, paired(gu, t))
                    for which in range(2):
                        rows = both[8 * which : 8 * which + 8]
                        for tile_at in range(2):
                            at = (t + tile_at) % 27 + 27 * which
                            put(1 + (t + tile_at) // 27, at, rows[:, tile_at * LANES : (tile_at + 1) * LANES])
                send_core(1 + half)
                if half == 0:
                    send_y(0)

        else:
            vs = [masked(6 + j) for j in range(4)]
            uq, uo = masked(10), masked(11)
            uk, uv = unmix(12)
            hash_among(MIX[3])
            three = nn(jnp.concatenate([uq, uk, uv], axis=0), xh[...])
            put(3, 0, three[:8])
            put(3, 10, nn(vs[0], gq[...]))
            put(3, 20, three[8:16])
            put(3, 32, three[16:])
            both = nn(mix([vs[1], vs[2]]), paired(kv, 0))
            put(3, 30, both[:8])
            put(3, 42, both[8:])
            put(3, 44, nn(uo, xo[...]))
            put(3, 54, nn(vs[3], go[...]))
            send_core(3)

    def send_z(chunk):
        wait_for(y_in.at[chunk], y_recv.at[chunk])
        if chunk == 0:
            pl.semaphore_wait(told_sem, 3)
        quarter[chunk] = (half[chunk, pl.ds(y * 8, 8)] + y_in[chunk, 0]) + (y_in[chunk, 1] + y_in[chunk, 2])
        for dx, dz in cross[::-1]:
            to_x, to_z = turn(x, dx, 4), turn(zh, dz, 2)
            remote(
                quarter.at[chunk, to_x * 2 + to_z], z_in.at[chunk, x * 2 + zh], z_send.at[chunk], z_recv.at[chunk],
                device(to_x, y, to_z, core, mp),
            )
        z_in[chunk, x * 2 + zh] = quarter[chunk, x * 2 + zh]

    def project(chunk):
        wait_for(z_in.at[chunk, pl.ds(0, 7)], z_recv.at[chunk])
        for example in range(4):
            g = z_in[chunk, 2 * example] + z_in[chunk, 2 * example + 1]
            lhs[chunk, pl.ds(example, 8, stride=8), :] = g
            lhs[chunk, pl.ds(4 + example, 8, stride=8), :] = g - g.astype(BF16).astype(F32)
        left = jnp.concatenate([lhs[chunk, pl.ds(8 * rank, 8), :] for rank in range(8)], axis=1).astype(BF16)
        for start in range(0, K, 512):
            product = nn(left, table[chunk * 1024 : (chunk + 1) * 1024, start : start + 512])
            lanes = slice(start, start + 512)
            if chunk == 0:
                total[:, lanes] = product
            else:
                total[:, lanes] += product

    hash_rows(16)
    factor_products(0)
    factor_products(1)
    pl.semaphore_wait(barrier, len(greet))
    send_part(0)
    send_part(1)
    factor_products(2)
    hash_rows(24)
    send_part(2)
    hash_rows(40)
    token_sums(0)
    token_sums(1)
    send_y(1)
    token_sums(2)
    send_y(2)
    hash_rows(46)
    send_y(3)
    hash_rows(62)
    send_z(0)
    hash_rows(88)
    send_z(1)
    send_z(2)
    hash_rows(96)
    send_z(3)
    hash_rows(120)
    project(0)
    project(1)
    project(2)
    hash_rows(128)
    project(3)

    scale_out = 1.0 / (LENGTH * math.sqrt(21845.0 * K))
    for number in range(16):
        lanes = slice(number * LANES, (number + 1) * LANES)
        a_out[number] = (total[0:4, lanes] + total[4:8, lanes]) * scale_out
    here = x * 4 + y
    for dx, dy in plane[::-1]:
        to_x, to_y = turn(x, dx, 4), turn(y, dy, 4)
        remote(
            a_out.at[to_x * 4 + to_y], a_in.at[here], fin_send.at[0], fin_recv.at[0], device(to_x, to_y, zh, core, mp)
        )
    a_in[here] = a_out[here]
    wait_for(a_in.at[pl.ds(0, 15)], fin_recv.at[0])
    there = mp * 4 + zh * 2 + core
    b_in[there] = jnp.sum(a_in[...], axis=0)
    for dm, dz, dc in column[::-1]:
        remote(
            b_in.at[there], b_in.at[there], fin_send.at[1], fin_recv.at[1],
            device(x, y, turn(zh, dz, 2), turn(core, dc, 2), turn(mp, dm, 4)),
        )
    wait_for(b_in.at[pl.ds(0, 15)], fin_recv.at[1])
    summed = jnp.sum(b_in[...], axis=0)
    out_ref[...] = pltpu.roll(summed, (LANES - there * 8) % LANES, 1)

    for group, (start, size) in enumerate(GROUPS):
        wait_for(part_in.at[:, pl.ds(start, size)], mp_send.at[group])
    for chunk in range(4):
        wait_for(core_in.at[chunk], core_send.at[chunk])
        wait_for(y_in.at[chunk], y_send.at[chunk])
        wait_for(z_in.at[chunk, pl.ds(0, 7)], z_send.at[chunk])
    wait_for(a_in.at[pl.ds(0, 15)], fin_send.at[0])
    wait_for(b_in.at[pl.ds(0, 15)], fin_send.at[1])


def shards(*args):
    args = list(args)
    args[14] = args[14].reshape(1, LANES)

    def like(number):
        return pltpu.VMEM(args[number].shape, args[number].dtype)

    scratch = [like(number) for number in range(15)]
    scratch[5] = pltpu.VMEM((2, LANES, 2, LANES), BF16)
    scratch[7] = pltpu.VMEM((54, LANES, 2, LANES), BF16)
    scratch.append(pltpu.SMEM((14,), I32))
    tile = (8, LANES)
    scratch += [
        pltpu.SMEM((32,), I32),
        pltpu.VMEM((8, K), I32),
        pltpu.VMEM((4096, K), BF16),
        pltpu.VMEM((14, *tile), F32),
        pltpu.VMEM((3, 14, *tile), F32),
        pltpu.VMEM((4, 64, *tile), F32),
        pltpu.VMEM((4, 32, *tile), F32),
        pltpu.VMEM((4, 32, *tile), F32),
        pltpu.VMEM((4, 3, 8, *tile), F32),
        pltpu.VMEM((4, 8, *tile), F32),
        pltpu.VMEM((4, 8, *tile), F32),
        pltpu.VMEM((4, 64, LANES), F32),
        pltpu.VMEM((8, K), F32),
        pltpu.VMEM((16, 4, LANES), F32),
        pltpu.VMEM((16, 4, LANES), F32),
        pltpu.VMEM((16, 4, LANES), F32),
        pltpu.SemaphoreType.DMA((16,)),
        pltpu.SemaphoreType.DMA((3,)),
        pltpu.SemaphoreType.DMA((3,)),
    ]
    scratch += [pltpu.SemaphoreType.DMA((4,)) for _ in range(6)]
    scratch += [pltpu.SemaphoreType.DMA((2,)) for _ in range(2)]
    scratch.append(pltpu.SemaphoreType.REGULAR)
    full = pl.pallas_call(
        kernel,
        out_shape=jax.ShapeDtypeStruct((4, LANES), F32),
        in_specs=[pl.BlockSpec(memory_space=pl.ANY)] * 16,
        out_specs=pl.BlockSpec(memory_space=pltpu.VMEM),
        scratch_shapes=scratch,
        compiler_params=pltpu.CompilerParams(collective_id=0, has_side_effects=True, vmem_limit_bytes=56 * 2**20),
    )(*args)
    return full[:, :8]


def solution(mesh):
    in_specs = (
        P("proj", "mp"), P("proj", "mp"), P("proj", "mp"), P("proj", "mp"), P("proj", "mp"), P("proj", None, "mp"),
        P("proj", "mp"), P("proj", None, "mp"), P("proj", "mp"), P(None, None, "mp"), P(None, "mp"), P(None, None, "mp"),
        P(None, None, "mp"), P(None, None, "mp"), P("proj"), P(),
    )
    return jax.shard_map(shards, mesh=mesh, in_specs=in_specs, out_specs=P(None, ("mp", "proj")), check_vma=False)
```

```python
import functools
import math

import jax
import jax.numpy as jnp
from jax import lax
from jax.experimental import pallas as pl
from jax.experimental.pallas import tpu as pltpu
from jax.sharding import PartitionSpec as P

K = 2048
LENGTH = 2048
LANES = 128
MESH = pl.DeviceIdType.MESH
F32, BF16, I32 = jnp.float32, jnp.bfloat16, jnp.int32


def wrap(value):
    return (value + 2**31) % 2**32 - 2**31


M1, M2 = -2048144789, -1028477387
SEED_STEP, ROW_STEP, COL_STEP = 1103515245, 668265263, -1640531535

CHUNKS = (
    ((12, 54, 0, 54), (13, 10, 0, 10)),
    ((9, 54, 0, 27), (11, 54, 0, 27), (8, 10, 0, 10)),
    ((9, 54, 27, 27), (11, 54, 27, 27), (10, 10, 0, 10)),
    tuple((segment, blocks, 0, blocks) for segment, blocks in enumerate((10, 10, 10, 2, 10, 2, 10, 10))),
)
GROUPS = ((0, 2), (2, 4), (6, 8))
ROWS = 64
STEPS = 4096 // ROWS
GU_UNROLL = 9
MIX_LOOP = 0
MIX = (0, 0, 0, 0)


def srl(value, count):
    return lax.shift_right_logical(value, jnp.int32(count))


def nt(a, b):
    return lax.dot_general(a, b, (((1,), (1,)), ((), ())), preferred_element_type=F32)


def nn(a, b):
    return jnp.dot(a, b, preferred_element_type=F32)


def kernel(
    xh_in, xo_in, xg_in, xd_in, gq_in, kv_in, go_in, gu_in, gd_in, ai_in, ad_in, ao_in, kvb_in, gub_in, mask_in, seed_in,
    out_ref,
    xh, xo, xg, xd, gq, kv, go, gu, gd, ai, ad, ao, kvb, gub, mask, seed,
    key_base, col_key, table, part, part_in, grads, core_in, half, y_in, quarter, z_in, lhs, total, a_out, a_in, b_in,
    load_sem, mp_send, mp_recv, core_send, core_recv, y_send, y_recv, z_send, z_recv, fin_send, fin_recv, told_sem,
):
    mp = lax.axis_index("mp")
    proj = lax.axis_index("proj")
    x, y, zh, core = proj // 16, (proj // 4) % 4, (proj // 2) % 2, proj % 2

    def device(x, y, zh, core, mp):
        return {"mp": mp, "proj": x * 16 + y * 4 + zh * 2 + core}

    def turn(value, by, size):
        return (value + by) % size

    plane = [(dx, dy) for dx in range(4) for dy in range(4) if dx or dy]
    column = [(dm, dz, dc) for dm in range(4) for dz in range(2) for dc in range(2) if dm or dz or dc]
    cross = [(dx, dz) for dx in range(4) for dz in range(2) if dx or dz]
    greet = [device(x, y, zh, core, turn(mp, step, 4)) for step in range(1, 4)]
    greet += [device(x, turn(y, step, 4), zh, core, mp) for step in range(1, 4)]
    greet += [device(turn(x, step, 4), y, zh, core, mp) for step in range(1, 4)]
    greet += [device(x, y, zh, 1 - core, mp), device(x, y, 1 - zh, core, 3 - mp)]
    barrier = pltpu.get_barrier_semaphore()
    for peer in greet:
        pl.semaphore_signal(barrier, inc=1, device_id=peer, device_id_type=MESH)

    def load(number, source, target):
        pltpu.make_async_copy(source, target, load_sem.at[number]).start()

    def loaded(number, target):
        pltpu.make_async_copy(target, target, load_sem.at[number]).wait()

    load(15, seed_in, seed)
    load(10, ad_in, ad)
    load(3, xd_in, xd)
    load(11, ao_in, ao)
    load(8, gd_in, gd)
    load(13, gub_in, gub)
    for tile in range(54):
        load(7, gu_in.at[:, :, tile * LANES : (tile + 1) * LANES], gu.at[tile])
    load(9, ai_in, ai)
    load(2, xg_in, xg)
    load(0, xh_in, xh)
    load(12, kvb_in, kvb)
    for tile in range(2):
        load(5, kv_in.at[:, :, tile * LANES : (tile + 1) * LANES], kv.at[tile])
    load(4, gq_in, gq)
    load(1, xo_in, xo)
    load(6, go_in, go)
    load(14, mask_in, mask)

    place = lax.broadcasted_iota(I32, (8, K), 1)
    q, m, i = place >> 7, (place >> 3) & 15, place & 7
    col = (((m >> 2) * 64 + q * 4 + (m & 3)) * 8 + i) * COL_STEP
    col_key[...] = col ^ srl(col, 16)

    loaded(15, seed)
    block = core * 32 + y * 8 + x * 2 + zh
    for chunk, segments in enumerate(CHUNKS):
        edge = 0
        first = jnp.int32(0)
        for segment, blocks, begin, count in segments:
            here = seed[segment] * SEED_STEP + (mp * blocks + begin + block - edge) * wrap(LANES * 8 * ROW_STEP)
            first = here if edge == 0 else jnp.where(block >= edge, here, first)
            edge += count
        for rank in range(8):
            key_base[chunk * 8 + rank] = first + wrap(rank * ROW_STEP)

    def hash_step(step, carry):
        del carry
        base = key_base[step // (LANES // ROWS)]
        row0 = (step % (LANES // ROWS)) * ROWS
        row = base + (lax.broadcasted_iota(I32, (ROWS, LANES), 0) + row0) * wrap(8 * ROW_STEP)
        row = row ^ srl(row, 16)
        at = pl.multiple_of(step * ROWS, ROWS)
        for tile in range(K // LANES):
            lanes = slice(tile * LANES, (tile + 1) * LANES)
            key = jnp.concatenate([col_key[:, lanes]] * (ROWS // 8), axis=0)
            h = (row ^ key) * M1
            h = h ^ srl(h, 13)
            h = h * M2
            high = srl(h, 16).astype(jnp.int16)
            low = h.astype(jnp.int16) ^ high
            carry8 = lax.shift_right_logical(low, jnp.int16(8)) + lax.shift_right_logical(high, jnp.int16(8))
            table[pl.ds(at, ROWS), lanes] = (low + high - jnp.int16(255) * carry8 - jnp.int16(510)).astype(BF16)
        return 0

    done = [0]

    def hash_rows(until):
        if until > done[0]:
            lax.fori_loop(done[0], until, hash_step, 0)
            done[0] = until

    def hash_among(count):
        for step in range(done[0], done[0] + count):
            hash_step(step, 0)
        done[0] += count

    pair = lax.broadcasted_iota(I32, (2 * LANES, LANES), 0)
    token = lax.broadcasted_iota(I32, (2 * LANES, LANES), 1)
    pick = [(pair == 2 * token + j).astype(F32).astype(BF16) for j in range(2)]
    odd = (lax.broadcasted_iota(I32, (8, 2 * LANES), 1) & 1) == 1

    def remote(source, target, send, recv, peer):
        pltpu.make_async_remote_copy(
            src_ref=source, dst_ref=target, send_sem=send, recv_sem=recv, device_id=peer, device_id_type=MESH
        ).start()

    def wait_for(ref, sem):
        pltpu.make_async_copy(ref, ref, sem).wait()

    def paired(buffer, tile):
        return jnp.concatenate(
            [buffer.at[tile].reshape(2 * LANES, LANES)[...], buffer.at[tile + 1].reshape(2 * LANES, LANES)[...]], axis=1
        )

    def send_part(group):
        start, size = GROUPS[group]
        for step in range(1, 4):
            remote(
                part.at[pl.ds(start, size)], part_in.at[step - 1, pl.ds(start, size)], mp_send.at[group], mp_recv.at[group],
                device(x, y, zh, core, turn(mp, step, 4)),
            )

    def factor_products(group):
        if group == 0:
            for number, ref in ((10, ad), (3, xd), (11, ao), (8, gd)):
                loaded(number, ref)
            part[0] = nt(ad[...], xd[...])
            part[1] = nt(ao[2], gd[...])
        elif group == 1:
            for number, ref in ((13, gub), (7, gu), (9, ai), (2, xg)):
                loaded(number, ref)
            both = nt(jnp.concatenate([ai[4], ai[5]], axis=0), xg[...])
            part[2] = both[:8]
            part[3] = both[8:]

            begin = done[0]
            done[0] += MIX_LOOP * (27 // GU_UNROLL)

            def add(step, acc):
                for extra in range(MIX_LOOP):
                    hash_step(begin + step * MIX_LOOP + extra, 0)
                for pair_at in range(GU_UNROLL):
                    tile = (step * GU_UNROLL + pair_at) * 2
                    lanes = pl.ds(pl.multiple_of(tile * LANES, 2 * LANES), 2 * LANES)
                    acc += nt(jnp.concatenate([gub[0, :, lanes], gub[1, :, lanes]], axis=0), paired(gu, tile))
                return acc

            acc = lax.fori_loop(0, 27 // GU_UNROLL, add, jnp.zeros((16, 2 * LANES), F32))
            both = jnp.where(odd, acc[8:], acc[:8])
            part[4] = both[:, :LANES]
            part[5] = both[:, LANES:]
        else:
            for number, ref in ((0, xh), (12, kvb), (5, kv), (4, gq), (1, xo), (6, go)):
                loaded(number, ref)
            three = nt(jnp.concatenate([ai[0], ai[1], ai[2]], axis=0), xh[...])
            for j in range(3):
                part[6 + j] = three[8 * j : 8 * j + 8]
            part[9] = nt(ai[3], xo[...])
            part[10] = nt(ao[0], gq[...])
            part[11] = nt(ao[1], go[...])
            acc = nt(jnp.concatenate([kvb[0], kvb[1]], axis=0), paired(kv, 0))
            both = jnp.where(odd, acc[8:], acc[:8])
            part[12] = both[:, :LANES]
            part[13] = both[:, LANES:]

    def put(chunk, at, value):
        for tile in range(value.shape[1] // LANES):
            grads[chunk, at + tile] = value[:, tile * LANES : (tile + 1) * LANES]

    def put_wide(chunk, at, left, right):
        for start in range(0, right.shape[1], 1280):
            width = min(1280, right.shape[1] - start)
            put(chunk, at + start // LANES, nn(left, right[:, start : start + width]))

    def send_core(chunk):
        remote(
            grads.at[chunk, pl.ds((1 - core) * 32, 32)], core_in.at[chunk], core_send.at[chunk], core_recv.at[chunk],
            device(x, y, zh, 1 - core, mp),
        )

    def send_y(chunk):
        wait_for(core_in.at[chunk], core_recv.at[chunk])
        half[chunk] = grads[chunk, pl.ds(core * 32, 32)] + core_in[chunk]
        for step in (2, 1, 3):
            to = turn(y, step, 4)
            remote(
                half.at[chunk, pl.ds(to * 8, 8)], y_in.at[chunk, step - 1], y_send.at[chunk], y_recv.at[chunk],
                device(x, to, zh, core, mp),
            )

    def token_sums(group):
        start, size = GROUPS[group]
        region = part_in.at[:, pl.ds(start, size)]
        wait_for(region, mp_recv.at[group])
        if group == 0:
            loaded(14, mask)
            for step in range(1, 4):
                pl.semaphore_signal(told_sem, inc=1, device_id=device(turn(x, step, 4), y, zh, core, mp), device_id_type=MESH)
        weights = mask[...].astype(F32)

        def tile(number):
            return (part[number] + part_in[0, number]) + (part_in[1, number] + part_in[2, number])

        def masked(number):
            return (weights * tile(number)).astype(BF16)

        def unmix(number):
            mixed = jnp.concatenate([tile(number), tile(number + 1)], axis=1).astype(BF16)
            return [(weights * nn(mixed, pick[j])).astype(BF16) for j in range(2)]

        def mix(values):
            return jnp.concatenate([nt(values[j], pick[j]) for j in range(2)], axis=0).astype(BF16)

        if group == 0:
            v, u = masked(0), masked(1)
            hash_among(MIX[0])
            put_wide(0, 0, u, xd)
            put_wide(0, 54, v, gd)
            send_core(0)
        elif group == 1:
            v = mix([masked(2), masked(3)])
            u = jnp.concatenate(unmix(4), axis=0)
            both = nn(u, xg[...])
            put(1, 54, both[:8])
            put(2, 54, both[8:])
            for half in range(2):
                hash_among(MIX[1 + half])
                for t in range(0, 28, 2) if half == 0 else range(28, 54, 2):
                    both = nn(v, paired(gu, t))
                    for which in range(2):
                        rows = both[8 * which : 8 * which + 8]
                        for tile_at in range(2):
                            at = (t + tile_at) % 27 + 27 * which
                            put(1 + (t + tile_at) // 27, at, rows[:, tile_at * LANES : (tile_at + 1) * LANES])
                send_core(1 + half)
                if half == 0:
                    send_y(0)

        else:
            vs = [masked(6 + j) for j in range(4)]
            uq, uo = masked(10), masked(11)
            uk, uv = unmix(12)
            hash_among(MIX[3])
            three = nn(jnp.concatenate([uq, uk, uv], axis=0), xh[...])
            put(3, 0, three[:8])
            put(3, 10, nn(vs[0], gq[...]))
            put(3, 20, three[8:16])
            put(3, 32, three[16:])
            both = nn(mix([vs[1], vs[2]]), paired(kv, 0))
            put(3, 30, both[:8])
            put(3, 42, both[8:])
            put(3, 44, nn(uo, xo[...]))
            put(3, 54, nn(vs[3], go[...]))
            send_core(3)

    def send_z(chunk):
        wait_for(y_in.at[chunk], y_recv.at[chunk])
        if chunk == 0:
            pl.semaphore_wait(told_sem, 3)
        quarter[chunk] = (half[chunk, pl.ds(y * 8, 8)] + y_in[chunk, 0]) + (y_in[chunk, 1] + y_in[chunk, 2])
        for dx, dz in cross[::-1]:
            to_x, to_z = turn(x, dx, 4), turn(zh, dz, 2)
            remote(
                quarter.at[chunk, to_x * 2 + to_z], z_in.at[chunk, x * 2 + zh], z_send.at[chunk], z_recv.at[chunk],
                device(to_x, y, to_z, core, mp),
            )
        z_in[chunk, x * 2 + zh] = quarter[chunk, x * 2 + zh]

    def project(chunk):
        wait_for(z_in.at[chunk, pl.ds(0, 7)], z_recv.at[chunk])
        for example in range(4):
            g = z_in[chunk, 2 * example] + z_in[chunk, 2 * example + 1]
            lhs[chunk, pl.ds(example, 8, stride=8), :] = g
            lhs[chunk, pl.ds(4 + example, 8, stride=8), :] = g - g.astype(BF16).astype(F32)
        left = jnp.concatenate([lhs[chunk, pl.ds(8 * rank, 8), :] for rank in range(8)], axis=1).astype(BF16)
        for start in range(0, K, 512):
            product = nn(left, table[chunk * 1024 : (chunk + 1) * 1024, start : start + 512])
            lanes = slice(start, start + 512)
            if chunk == 0:
                total[:, lanes] = product
            else:
                total[:, lanes] += product

    hash_rows(8)
    factor_products(0)
    factor_products(1)
    pl.semaphore_wait(barrier, len(greet))
    send_part(0)
    send_part(1)
    factor_products(2)
    hash_rows(12)
    send_part(2)
    hash_rows(20)
    token_sums(0)
    token_sums(1)
    send_y(1)
    token_sums(2)
    send_y(2)
    hash_rows(23)
    send_y(3)
    hash_rows(31)
    send_z(0)
    hash_rows(44)
    send_z(1)
    send_z(2)
    hash_rows(48)
    send_z(3)
    hash_rows(60)
    project(0)
    project(1)
    project(2)
    hash_rows(64)
    project(3)

    scale_out = 1.0 / (LENGTH * math.sqrt(21845.0 * K))
    for number in range(16):
        lanes = slice(number * LANES, (number + 1) * LANES)
        a_out[number] = (total[0:4, lanes] + total[4:8, lanes]) * scale_out
    here = x * 4 + y
    for dx, dy in plane[::-1]:
        to_x, to_y = turn(x, dx, 4), turn(y, dy, 4)
        remote(
            a_out.at[to_x * 4 + to_y], a_in.at[here], fin_send.at[0], fin_recv.at[0], device(to_x, to_y, zh, core, mp)
        )
    a_in[here] = a_out[here]
    wait_for(a_in.at[pl.ds(0, 15)], fin_recv.at[0])
    there = mp * 4 + zh * 2 + core
    b_in[there] = jnp.sum(a_in[...], axis=0)
    for dm, dz, dc in column[::-1]:
        remote(
            b_in.at[there], b_in.at[there], fin_send.at[1], fin_recv.at[1],
            device(x, y, turn(zh, dz, 2), turn(core, dc, 2), turn(mp, dm, 4)),
        )
    wait_for(b_in.at[pl.ds(0, 15)], fin_recv.at[1])
    summed = jnp.sum(b_in[...], axis=0)
    out_ref[...] = pltpu.roll(summed, (LANES - there * 8) % LANES, 1)

    for group, (start, size) in enumerate(GROUPS):
        wait_for(part_in.at[:, pl.ds(start, size)], mp_send.at[group])
    for chunk in range(4):
        wait_for(core_in.at[chunk], core_send.at[chunk])
        wait_for(y_in.at[chunk], y_send.at[chunk])
        wait_for(z_in.at[chunk, pl.ds(0, 7)], z_send.at[chunk])
    wait_for(a_in.at[pl.ds(0, 15)], fin_send.at[0])
    wait_for(b_in.at[pl.ds(0, 15)], fin_send.at[1])


def shards(*args):
    args = list(args)
    args[14] = args[14].reshape(1, LANES)

    def like(number):
        return pltpu.VMEM(args[number].shape, args[number].dtype)

    scratch = [like(number) for number in range(15)]
    scratch[5] = pltpu.VMEM((2, LANES, 2, LANES), BF16)
    scratch[7] = pltpu.VMEM((54, LANES, 2, LANES), BF16)
    scratch.append(pltpu.SMEM((14,), I32))
    tile = (8, LANES)
    scratch += [
        pltpu.SMEM((32,), I32),
        pltpu.VMEM((8, K), I32),
        pltpu.VMEM((4096, K), BF16),
        pltpu.VMEM((14, *tile), F32),
        pltpu.VMEM((3, 14, *tile), F32),
        pltpu.VMEM((4, 64, *tile), F32),
        pltpu.VMEM((4, 32, *tile), F32),
        pltpu.VMEM((4, 32, *tile), F32),
        pltpu.VMEM((4, 3, 8, *tile), F32),
        pltpu.VMEM((4, 8, *tile), F32),
        pltpu.VMEM((4, 8, *tile), F32),
        pltpu.VMEM((4, 64, LANES), F32),
        pltpu.VMEM((8, K), F32),
        pltpu.VMEM((16, 4, LANES), F32),
        pltpu.VMEM((16, 4, LANES), F32),
        pltpu.VMEM((16, 4, LANES), F32),
        pltpu.SemaphoreType.DMA((16,)),
        pltpu.SemaphoreType.DMA((3,)),
        pltpu.SemaphoreType.DMA((3,)),
    ]
    scratch += [pltpu.SemaphoreType.DMA((4,)) for _ in range(6)]
    scratch += [pltpu.SemaphoreType.DMA((2,)) for _ in range(2)]
    scratch.append(pltpu.SemaphoreType.REGULAR)
    full = pl.pallas_call(
        kernel,
        out_shape=jax.ShapeDtypeStruct((4, LANES), F32),
        in_specs=[pl.BlockSpec(memory_space=pl.ANY)] * 16,
        out_specs=pl.BlockSpec(memory_space=pltpu.VMEM),
        scratch_shapes=scratch,
        compiler_params=pltpu.CompilerParams(collective_id=0, has_side_effects=True, vmem_limit_bytes=56 * 2**20),
    )(*args)
    return full[:, :8]


def solution(mesh):
    in_specs = (
        P("proj", "mp"), P("proj", "mp"), P("proj", "mp"), P("proj", "mp"), P("proj", "mp"), P("proj", None, "mp"),
        P("proj", "mp"), P("proj", None, "mp"), P("proj", "mp"), P(None, None, "mp"), P(None, "mp"), P(None, None, "mp"),
        P(None, None, "mp"), P(None, None, "mp"), P("proj"), P(),
    )
    return jax.shard_map(shards, mesh=mesh, in_specs=in_specs, out_specs=P(None, ("mp", "proj")), check_vma=False)
```
